32 devices in a mesh: grp: 2 (over y), grid: 4 (over z), rep: 4 (over x, core).
Axes of the slice: x: 2, y: 2, z: 4, core: 2. Of those that a mesh axis runs over, the one named last changes fastest.
Arguments:
- task_blocks: float32 [48, 8, 128, 128], P(('grp', 'grid'), 'rep'), parts along dimension 0, may hold values from -1.75 to 1.75
- block_cols: int32 [48, 8], P('grp'), parts along dimension 0, may hold values from 0 to 23, as said below
- task_slot: int32 [48, 8], P('grp'), parts along dimension 0, may hold values from 0 to 7, each once within a row
Outputs:
- purified: float32 [48, 8, 128, 128], P(('grp', 'grid'), 'rep'), parts along dimension 0
The draws below stay inside these ranges and needn't reach their ends.
There are 2 independent parts, one for each index of `grp`. The reference program is written for one: setup_inputs(seed, part) draws one part's arguments, and reference() takes and returns one part's arrays. A program takes and returns all parts, laid end to end along the dimension named above; each array names one. Nothing has to cross between parts.
Inputs may be any that keep to these rules, and one draw needn't show every extreme that they name: `block_cols`: the 8 block columns of a block row are distinct, the first is the row itself, and all lie among the block rows of the row's index of grid and of the two indices beside it, wrapping around: block row i of index g = i // 6 names columns ((6 * (g - 1) + c) mod 24) for c below 18.
All inputs are finite; a program needn't handle non-finite values.
Results may differ from the reference program's by a relative error of at most 0.00011.
Values sent between devices are 32-bit elements; how exact they have to be, the bound alone decides.
A program may use at most 64 MiB of HBM per device.

```python
import jax
import jax.numpy as jnp
from jax import lax

BS = 128
NZR = 8
ROWS = 6
NB = 24


def draw_block_cols(key, part):
    key = jax.random.fold_in(key, 11)
    row_ids = jnp.arange(NB, dtype=jnp.int32)
    owners = row_ids // ROWS
    offsets = jnp.arange(3 * ROWS, dtype=jnp.int32)
    candidates = (ROWS * (owners[:, None] - 1) + offsets[None, :]) % NB
    own_place = row_ids % ROWS + ROWS
    scores = jax.random.randint(key, (NB, 3 * ROWS), 0, 1048576, dtype=jnp.int32) * (3 * ROWS) + offsets[None, :]
    scores = jnp.where(offsets[None, :] == own_place[:, None], -1, scores)
    order = jnp.argsort(scores, axis=1, stable=True)[:, :NZR]
    return jnp.take_along_axis(candidates, order, axis=1).astype(jnp.int32)


def levels(rng, shape, split, smallest, top_value):
    loudness, own = 1.0, jax.random.fold_in(rng, 6)
    for position, shards_of in split:
        draws = jnp.exp(jax.random.uniform(jax.random.fold_in(own, position), (shards_of,), jnp.float32, smallest / len(split), top_value / len(split)))
        loudness = loudness * jnp.repeat(draws, shape[position] // shards_of).reshape([-1 if axis == position else 1 for axis in range(len(shape))])
    return loudness


def gaussian(key, extent, width, bound, cuts=(), kind=jnp.bfloat16):
    array = width * jax.random.normal(key, extent, jnp.float32)
    if cuts:
        array = array * levels(key, extent, cuts, -0.22, 0.18)
    return jnp.clip(array, -bound, bound).astype(kind)


def setup_inputs(seed: int = 0, part: int = 0) -> dict:
    key_list = jax.random.split(jax.random.key(seed), 4)
    own_keys = jax.random.split(jax.random.fold_in(key_list[3], part), 4)
    return {
        "task_blocks": gaussian(own_keys[0], (NB, NZR, BS, BS), 0.12, 1.75, ((0, 4), (1, 4)), jnp.float32),
        "block_cols": draw_block_cols(jax.random.fold_in(jax.random.fold_in(key_list[3], part), 71), part),
        "task_slot": jax.vmap(lambda own: jax.random.permutation(own, NZR))(jax.random.split(own_keys[2], NB)).reshape((NB, NZR)).astype(jnp.int32),
    }


def reference(task_blocks, block_cols, task_slot):
    slot_ids = jnp.arange(NZR, dtype=jnp.int32)
    inverse = jnp.sum(jnp.where(task_slot[:, :, None] == slot_ids[None, None, :], slot_ids[None, :, None], 0), axis=1).astype(jnp.int32)
    density = jnp.take_along_axis(task_blocks, inverse[:, :, None, None], axis=1)
    inner_cols = block_cols[block_cols]
    matches = inner_cols[:, :, None, :] == block_cols[:, None, :, None]
    present = jnp.any(matches, axis=-1)
    chosen = jnp.argmax(matches.astype(jnp.int32), axis=-1).astype(jnp.int32)
    flat_blocks = density.reshape(NB * NZR, BS, BS)
    lookup = (block_cols[:, :, None] * NZR + chosen).astype(jnp.int32)

    def one_row(operand):
        block_row, row_lookup, row_present = operand
        partner = jnp.take(flat_blocks, row_lookup.reshape(-1), axis=0).reshape(NZR, NZR, BS, BS)
        partner = partner * row_present[:, :, None, None].astype(jnp.float32)
        square = jnp.einsum('kab,kmbc->mac', block_row, partner, precision=lax.Precision.HIGHEST)
        cubed = jnp.einsum('kab,kmbc->mac', square, partner, precision=lax.Precision.HIGHEST)
        return 3.0 * square - 2.0 * cubed

    return lax.map(one_row, (density, lookup, present))
```

```python
import functools

import jax
import jax.numpy as jnp
from jax import lax
from jax.experimental import pallas as pl
from jax.experimental.pallas import tpu as pltpu
from jax.sharding import PartitionSpec as P

MESH = pl.DeviceIdType.MESH


def lookup_tables(block_cols, task_slot, row_count):
    block_total, slot_count = block_cols.shape
    grid_place = lax.axis_index("grid")
    first_row = row_count * (grid_place - 1)
    near_count = 3 * row_count
    near_ids = (first_row + jnp.arange(near_count, dtype=jnp.int32)) % block_total
    near_cols = block_cols[near_ids]
    near_slot = task_slot[near_ids]
    slots = jnp.arange(slot_count, dtype=jnp.int32)
    hot = near_slot[:, :, None] == slots[None, None, :]
    near_task = jnp.sum(jnp.where(hot, near_cols[:, None, :], 0), axis=2)
    own_cols = near_cols[row_count : 2 * row_count]
    own_task = near_task[row_count : 2 * row_count]
    places = jnp.arange(near_count, dtype=jnp.int32)
    tile = (
        (places // row_count)[:, None] * (slot_count // 2) + slots[None, :] // 2
    ) * row_count + (places % row_count)[:, None]
    code = 4 * tile + slots[None, :] % 2
    match = near_task[None, :, None, :] == own_cols[:, None, :, None]
    found = 2 + jnp.sum(jnp.where(match, code[None, :, None, :] - 2, 0), axis=3)
    left_cols = jnp.stack([own_task, own_cols])
    left_place = (left_cols - first_row) % block_total
    pick = left_place[:, :, :, None] == places
    table = jnp.sum(jnp.where(pick[..., None], found[None, :, None], 0), axis=3)
    return table.reshape(2, -1)


def kernel(
    grid_size, table, task_ref, out_ref,
    own, stage, left, near, near_hi, near_lo, square, out_stage, landed,
    task_sem, z_send, z_recv, x_send, x_recv, s_send, s_recv,
    l_send, l_recv, q_send, q_recv, o_send, o_recv,
):
    row_count, _, size, _ = own.shape
    half = size // 2
    slot_count = 2 * left.shape[0]
    grid_place = lax.axis_index("grid")
    rep = lax.axis_index("rep")
    side = rep // 2
    part = rep % 2
    sib = 2 * side + 1 - part
    ctr = 2 * (1 - side) + part
    diag = 2 * (1 - side) + 1 - part
    up = lax.rem(grid_place + 1, grid_size)
    down = lax.rem(grid_place + grid_size - 1, grid_size)

    def remote(src, dst, send, recv, **where):
        return pltpu.make_async_remote_copy(
            src_ref=src, dst_ref=dst, send_sem=send, recv_sem=recv,
            device_id=where, device_id_type=MESH,
        )

    fetch = pltpu.make_async_copy(task_ref, own, task_sem)
    fetch.start()
    barrier = pltpu.get_barrier_semaphore()
    for where in ({"grid": up}, {"grid": down}, {"rep": sib}, {"rep": ctr}, {"rep": diag}):
        pl.semaphore_signal(barrier, inc=1, device_id=where, device_id_type=MESH)
    fetch.wait()

    low_lanes = lax.broadcasted_iota(jnp.int32, (size, size), 1) < half

    def swap(first, second):
        low = low_lanes[: first.shape[0]]
        return (
            jnp.where(low, first, pltpu.roll(second, half, 1)),
            jnp.where(low, pltpu.roll(first, half, 1), second),
        )

    @pl.loop(0, row_count)
    def _(i):
        packed = swap(own[i, 0], own[i, 1])
        near[1, rep, i] = jnp.where(side == 0, packed[0], packed[1])
        stage[i] = jnp.where(side == 0, packed[1], packed[0])

    pl.semaphore_wait(barrier, 5)

    to_ctr = remote(stage, near.at[1, rep], x_send, x_recv, rep=ctr)
    to_ctr.start()

    def z_copy(n, source):
        return remote(
            near.at[1, source], near.at[2 * (n % 2), source],
            z_send.at[n], z_recv.at[n], grid=up if n % 2 == 0 else down,
        )

    z_own = [z_copy(n, rep) for n in (0, 1)]
    for copy in z_own:
        copy.start()

    def s_copy(n, direction, source):
        return remote(
            near.at[direction, source], near.at[direction, source],
            s_send.at[n], s_recv.at[n], rep=sib,
        )

    s_copies = [
        s_copy(0, 1, rep), s_copy(1, 1, ctr), s_copy(2, 0, rep),
        s_copy(3, 2, rep), s_copy(4, 0, ctr), s_copy(5, 2, ctr),
    ]
    s_copies[0].start()

    def left_rows(which):
        return own.at[:, :, pl.ds(pl.multiple_of(which * half, half), half), :]

    lefts = [
        remote(left_rows(1 - part), left.at[rep], l_send.at[0], l_recv.at[0], rep=sib),
        remote(left_rows(part), left.at[rep], l_send.at[1], l_recv.at[1], rep=ctr),
        remote(left_rows(1 - part), left.at[rep], l_send.at[2], l_recv.at[2], rep=diag),
    ]
    lefts[0].start()

    @pl.loop(0, row_count)
    def _(i):
        for n in range(2):
            left[rep, i, n] = own[i, n, pl.ds(pl.multiple_of(part * half, half), half), :]

    def split(value):
        high = value.astype(jnp.bfloat16)
        return high, (value - high.astype(jnp.float32)).astype(jnp.bfloat16)

    def convert(direction, source):
        base = (direction * (slot_count // 2) + source) * row_count

        @pl.loop(0, row_count)
        def _(i):
            high, low = split(near[direction, source, i])
            near_hi[base + i] = high
            near_lo[base + i] = low

    convert(1, rep)
    to_ctr.wait_recv()
    z_ctr = [z_copy(n, ctr) for n in (2, 3)]
    for copy in z_ctr:
        copy.start()
    s_copies[1].start()
    to_ctr.wait_send()
    lefts[1].start()
    lefts[2].start()
    convert(1, ctr)
    s_copies[0].wait_recv()
    convert(1, sib)
    s_copies[1].wait_recv()
    convert(1, diag)
    for copy, onward, direction in zip(z_own, s_copies[2:4], (0, 2)):
        copy.wait_recv()
        onward.start()
        convert(direction, rep)
    for onward, direction in zip(s_copies[2:4], (0, 2)):
        onward.wait_recv()
        convert(direction, sib)
    for copy in lefts:
        copy.wait_recv()
    for copy, onward, direction in zip(z_ctr, s_copies[4:6], (0, 2)):
        copy.wait_recv()
        onward.start()
        convert(direction, ctr)
    for onward, direction in zip(s_copies[4:6], (0, 2)):
        onward.wait_recv()
        convert(direction, diag)

    lane_half = lax.broadcasted_iota(jnp.int32, (size, size), 1) // half
    nothing = jnp.zeros((size, size), jnp.bfloat16)

    def products(which, i, pair, lhs):
        total = jnp.zeros((half, 2 * size), jnp.float32)
        for s in range(0, slot_count, 2):
            highs, lows = [], []
            for t in (s, s + 1):
                high_row, low_row = [], []
                for m in range(2):
                    code = table[which, (i * slot_count + t) * slot_count + 2 * pair + m]
                    tile = code // 4
                    keep = lane_half == code % 4
                    high_row.append(jnp.where(keep, near_hi[tile], nothing))
                    low_row.append(jnp.where(keep, near_lo[tile], nothing))
                highs.append(jnp.concatenate(high_row, axis=1))
                lows.append(jnp.concatenate(low_row, axis=1))
            both = lhs[:, s * size : (s + 2) * size]
            wide = jnp.dot(
                both, jnp.concatenate(highs, axis=0), preferred_element_type=jnp.float32
            )
            total += wide[:half] + wide[half:] + jnp.dot(
                both[:half], jnp.concatenate(lows, axis=0), preferred_element_type=jnp.float32
            )
        first, second = total[:, :size], total[:, size:]
        return jnp.where(
            low_lanes[:half], first + pltpu.roll(first, half, 1), second + pltpu.roll(second, half, 1)
        )

    def left_operand(tiles):
        high, low = split(jnp.concatenate(tiles, axis=1))
        return jnp.concatenate([high, low], axis=0)

    def square_copy(i):
        return remote(
            square.at[side, i], square.at[side, i], q_send.at[i], q_recv.at[i], rep=ctr
        )

    @pl.loop(0, row_count)
    def _(i):
        lhs = left_operand([left[t // 2, i, t % 2] for t in range(slot_count)])
        for pair in range(slot_count // 2):
            square[side, i, pair] = products(0, i, pair, lhs)
        square_copy(i).start()

    def out_copy(i, n, peer):
        return remote(
            out_stage.at[i, peer],
            landed.at[side, i, pl.ds(pl.multiple_of(part * half, half), half), :],
            o_send.at[n, i], o_recv.at[n, i], rep=peer,
        )

    peers = (diag, ctr, sib)

    @pl.loop(0, row_count)
    def _(i):
        square_copy(i).wait_recv()
        tiles = []
        for pair in range(slot_count // 2):
            tiles.extend(swap(square[0, i, pair], square[1, i, pair]))
        lhs = left_operand(tiles)
        for pair in range(slot_count // 2):
            cubed = products(1, i, pair, lhs)
            out_stage[i, pair] = 3.0 * square[side, i, pair] - 2.0 * cubed
        for n, peer in enumerate(peers):
            out_copy(i, n, peer).start()
        landed[side, i, pl.ds(pl.multiple_of(part * half, half), half), :] = out_stage[i, rep]

    @pl.loop(0, row_count)
    def _(i):
        for n, peer in enumerate(peers):
            out_copy(i, n, peer).wait_recv()
        first, second = swap(landed[0, i], landed[1, i])
        out_ref[i, 0] = first
        out_ref[i, 1] = second

    for copy in z_own + z_ctr + s_copies + lefts:
        copy.wait_send()

    @pl.loop(0, row_count)
    def _(i):
        square_copy(i).wait_send()
        for n, peer in enumerate(peers):
            out_copy(i, n, peer).wait_send()


def local(grid_size, rep_size, task_blocks, block_cols, task_slot):
    row_count, slots_here, size, _ = task_blocks.shape
    pairs = rep_size
    table = lookup_tables(block_cols, task_slot, row_count)
    half = size // 2
    f32, bf16 = jnp.float32, jnp.bfloat16
    dma = pltpu.SemaphoreType.DMA
    return pl.pallas_call(
        functools.partial(kernel, grid_size),
        out_shape=jax.ShapeDtypeStruct(task_blocks.shape, f32),
        in_specs=[
            pl.BlockSpec(memory_space=pltpu.SMEM),
            pl.BlockSpec(memory_space=pl.ANY),
        ],
        out_specs=pl.BlockSpec(memory_space=pltpu.VMEM),
        scratch_shapes=[
            pltpu.VMEM((row_count, slots_here, size, size), f32),
            pltpu.VMEM((row_count, size, size), f32),
            pltpu.VMEM((rep_size, row_count, slots_here, half, size), f32),
            pltpu.VMEM((3, rep_size, row_count, size, size), f32),
            pltpu.VMEM((3 * rep_size * row_count, size, size), bf16),
            pltpu.VMEM((3 * rep_size * row_count, size, size), bf16),
            pltpu.VMEM((2, row_count, pairs, half, size), f32),
            pltpu.VMEM((row_count, pairs, half, size), f32),
            pltpu.VMEM((2, row_count, size, size), f32),
            dma, dma((4,)), dma((4,)), dma, dma, dma((6,)), dma((6,)),
            dma((3,)), dma((3,)), dma((row_count,)), dma((row_count,)),
            dma((3, row_count)), dma((3, row_count)),
        ],
        compiler_params=pltpu.CompilerParams(
            collective_id=0, has_side_effects=True, vmem_limit_bytes=40 * 1024 * 1024
        ),
    )(table, task_blocks)


def solution(mesh):
    return jax.shard_map(
        functools.partial(local, mesh.shape["grid"], mesh.shape["rep"]),
        mesh=mesh,
        in_specs=(P(("grp", "grid"), "rep", None, None), P("grp", None), P("grp", None)),
        out_specs=P(("grp", "grid"), "rep", None, None),
        check_vma=False,
    )
```

```python
import functools

import jax
import jax.numpy as jnp
from jax import lax
from jax.experimental import pallas as pl
from jax.experimental.pallas import tpu as pltpu
from jax.sharding import PartitionSpec as P

MESH = pl.DeviceIdType.MESH


def kernel(
    grid_size, task_ref, cols_ref, slots_ref, out_ref,
    cols, slots, cols_smem, slots_smem, near_cols, near_slots, codes_vmem, codes,
    own, stage, left, near, near_hi, near_lo, square, out_stage, landed,
    task_sem, meta_sem, z_send, z_recv, x_send, x_recv, s_send, s_recv,
    l_send, l_recv, q_send, q_recv, o_send, o_recv,
):
    row_count, _, size, _ = own.shape
    half = size // 2
    slot_count = 2 * left.shape[0]
    grid_place = lax.axis_index("grid")
    rep = lax.axis_index("rep")
    side = rep // 2
    part = rep % 2
    sib = 2 * side + 1 - part
    ctr = 2 * (1 - side) + part
    diag = 2 * (1 - side) + 1 - part
    up = lax.rem(grid_place + 1, grid_size)
    down = lax.rem(grid_place + grid_size - 1, grid_size)

    def remote(src, dst, send, recv, **where):
        return pltpu.make_async_remote_copy(
            src_ref=src, dst_ref=dst, send_sem=send, recv_sem=recv,
            device_id=where, device_id_type=MESH,
        )

    fetch = pltpu.make_async_copy(task_ref, own, task_sem)
    fetch.start()
    meta = [
        pltpu.make_async_copy(src, dst, meta_sem.at[n])
        for n, (src, dst) in enumerate((
            (cols_ref, cols), (slots_ref, slots), (cols_ref, cols_smem), (slots_ref, slots_smem)
        ))
    ]
    for copy in meta:
        copy.start()
    barrier = pltpu.get_barrier_semaphore()
    for where in ({"grid": up}, {"grid": down}, {"rep": sib}, {"rep": ctr}, {"rep": diag}):
        pl.semaphore_signal(barrier, inc=1, device_id=where, device_id_type=MESH)
    fetch.wait()

    low_lanes = lax.broadcasted_iota(jnp.int32, (size, size), 1) < half

    def swap(first, second):
        low = low_lanes[: first.shape[0]]
        return (
            jnp.where(low, first, pltpu.roll(second, half, 1)),
            jnp.where(low, pltpu.roll(first, half, 1), second),
        )

    @pl.loop(0, row_count)
    def _(i):
        packed = swap(own[i, 0], own[i, 1])
        near[1, rep, i] = jnp.where(side == 0, packed[0], packed[1])
        stage[i] = jnp.where(side == 0, packed[1], packed[0])

    pl.semaphore_wait(barrier, 5)

    to_ctr = remote(stage, near.at[1, rep], x_send, x_recv, rep=ctr)
    to_ctr.start()

    def z_copy(n, source):
        return remote(
            near.at[1, source], near.at[2 * (n % 2), source],
            z_send.at[n], z_recv.at[n], grid=up if n % 2 == 0 else down,
        )

    z_own = [z_copy(n, rep) for n in (0, 1)]
    for copy in z_own:
        copy.start()

    def s_copy(n, direction, source):
        return remote(
            near.at[direction, source], near.at[direction, source],
            s_send.at[n], s_recv.at[n], rep=sib,
        )

    s_copies = [
        s_copy(0, 1, rep), s_copy(1, 1, ctr), s_copy(2, 0, rep),
        s_copy(3, 2, rep), s_copy(4, 0, ctr), s_copy(5, 2, ctr),
    ]
    s_copies[0].start()

    def left_rows(which):
        return own.at[:, :, pl.ds(pl.multiple_of(which * half, half), half), :]

    lefts = [
        remote(left_rows(1 - part), left.at[rep], l_send.at[0], l_recv.at[0], rep=sib),
        remote(left_rows(part), left.at[rep], l_send.at[1], l_recv.at[1], rep=ctr),
        remote(left_rows(1 - part), left.at[rep], l_send.at[2], l_recv.at[2], rep=diag),
    ]
    lefts[0].start()

    @pl.loop(0, row_count)
    def _(i):
        for n in range(2):
            left[rep, i, n] = own[i, n, pl.ds(pl.multiple_of(part * half, half), half), :]

    def split(value):
        high = value.astype(jnp.bfloat16)
        return high, (value - high.astype(jnp.float32)).astype(jnp.bfloat16)

    def convert(direction, source):
        base = (direction * (slot_count // 2) + source) * row_count

        @pl.loop(0, row_count)
        def _(i):
            high, low = split(near[direction, source, i])
            near_hi[base + i] = high
            near_lo[base + i] = low

    for copy in meta:
        copy.wait()
    pad = near_cols.shape[0] // 3
    for d in range(3):
        start = row_count * lax.rem(grid_place + grid_size + d - 1, grid_size)
        for i in range(row_count):
            near_cols[pl.ds(d * pad + i, 1), :] = cols[pl.ds(start + i, 1), :]
            near_slots[pl.ds(d * pad + i, 1), :] = slots[pl.ds(start + i, 1), :]
    rows = lax.broadcasted_iota(jnp.int32, near_cols.shape, 0)
    slot_ids = lax.broadcasted_iota(jnp.int32, near_cols.shape, 1)
    by_col, by_task = near_cols[...], near_slots[...]
    tile = (rows // pad) * (slot_count // 2) * row_count + rows % pad
    last_code = 4 * near_hi.shape[0] - 1
    coded = jnp.zeros(near_cols.shape, jnp.int32)
    for t in range(slot_count):
        coded += jnp.where(
            by_task[:, t : t + 1] == slot_ids, 4 * (tile + (t // 2) * row_count) + t % 2 - 2, 0
        )
    for i in range(row_count):
        mine = near_cols[pl.ds(pad + i, 1), :]
        found = jnp.full(near_cols.shape, 2, jnp.int32)
        for n in range(slot_count):
            found += jnp.where(by_col[:, n : n + 1] == mine, coded[:, n : n + 1], 0)
        codes_vmem[:, i * slot_count : (i + 1) * slot_count] = jnp.clip(found, 0, last_code)
    to_smem = pltpu.make_async_copy(codes_vmem, codes, meta_sem.at[4])
    to_smem.start()
    convert(1, rep)
    to_smem.wait()
    to_ctr.wait_recv()
    z_ctr = [z_copy(n, ctr) for n in (2, 3)]
    for copy in z_ctr:
        copy.start()
    s_copies[1].start()
    to_ctr.wait_send()
    lefts[1].start()
    lefts[2].start()
    convert(1, ctr)
    s_copies[0].wait_recv()
    convert(1, sib)
    s_copies[1].wait_recv()
    convert(1, diag)
    for copy, onward, direction in zip(z_own, s_copies[2:4], (0, 2)):
        copy.wait_recv()
        onward.start()
        convert(direction, rep)
    for onward, direction in zip(s_copies[2:4], (0, 2)):
        onward.wait_recv()
        convert(direction, sib)
    for copy in lefts:
        copy.wait_recv()
    for copy, onward, direction in zip(z_ctr, s_copies[4:6], (0, 2)):
        copy.wait_recv()
        onward.start()
        convert(direction, ctr)
    for onward, direction in zip(s_copies[4:6], (0, 2)):
        onward.wait_recv()
        convert(direction, diag)

    lane_half = lax.broadcasted_iota(jnp.int32, (size, size), 1) // half
    nothing = jnp.zeros((size, size), jnp.bfloat16)

    first_row = row_count * (grid_place - 1)
    block_total = row_count * grid_size

    def near_place(i, s, in_task_order):
        row = row_count * grid_place + i
        slot = slots_smem[row, s] if in_task_order else s
        place = cols_smem[row, slot] - first_row
        place = jnp.where(place < 0, place + block_total, place)
        place = jnp.where(place >= block_total, place - block_total, place)
        place = jnp.clip(place, 0, 3 * row_count - 1)
        return place + (pad - row_count) * (place // row_count)

    def products(places, i, pair, lhs):
        total = jnp.zeros((half, 2 * size), jnp.float32)
        for s in range(0, slot_count, 2):
            highs, lows = [], []
            for t in (s, s + 1):
                high_row, low_row = [], []
                for m in range(2):
                    code = codes[places[t], i * slot_count + 2 * pair + m]
                    tile = code // 4
                    keep = lane_half == code % 4
                    high_row.append(jnp.where(keep, near_hi[tile], nothing))
                    low_row.append(jnp.where(keep, near_lo[tile], nothing))
                highs.append(jnp.concatenate(high_row, axis=1))
                lows.append(jnp.concatenate(low_row, axis=1))
            both = lhs[:, s * size : (s + 2) * size]
            wide = jnp.dot(
                both, jnp.concatenate(highs, axis=0), preferred_element_type=jnp.float32
            )
            total += wide[:half] + wide[half:] + jnp.dot(
                both[:half], jnp.concatenate(lows, axis=0), preferred_element_type=jnp.float32
            )
        first, second = total[:, :size], total[:, size:]
        return jnp.where(
            low_lanes[:half], first + pltpu.roll(first, half, 1), second + pltpu.roll(second, half, 1)
        )

    def left_operand(tiles):
        high, low = split(jnp.concatenate(tiles, axis=1))
        return jnp.concatenate([high, low], axis=0)

    def square_copy(i):
        return remote(
            square.at[side, i], square.at[side, i], q_send.at[i], q_recv.at[i], rep=ctr
        )

    @pl.loop(0, row_count)
    def _(i):
        places = [near_place(i, s, True) for s in range(slot_count)]
        lhs = left_operand([left[t // 2, i, t % 2] for t in range(slot_count)])
        for pair in range(slot_count // 2):
            square[side, i, pair] = products(places, i, pair, lhs)
        square_copy(i).start()

    def out_copy(i, n, peer):
        return remote(
            out_stage.at[i, peer],
            landed.at[side, i, pl.ds(pl.multiple_of(part * half, half), half), :],
            o_send.at[n, i], o_recv.at[n, i], rep=peer,
        )

    peers = (diag, ctr, sib)

    @pl.loop(0, row_count)
    def _(i):
        square_copy(i).wait_recv()
        places = [near_place(i, s, False) for s in range(slot_count)]
        tiles = []
        for pair in range(slot_count // 2):
            tiles.extend(swap(square[0, i, pair], square[1, i, pair]))
        lhs = left_operand(tiles)
        for pair in range(slot_count // 2):
            cubed = products(places, i, pair, lhs)
            out_stage[i, pair] = 3.0 * square[side, i, pair] - 2.0 * cubed
        for n, peer in enumerate(peers):
            out_copy(i, n, peer).start()
        landed[side, i, pl.ds(pl.multiple_of(part * half, half), half), :] = out_stage[i, rep]

    @pl.loop(0, row_count)
    def _(i):
        for n, peer in enumerate(peers):
            out_copy(i, n, peer).wait_recv()
        first, second = swap(landed[0, i], landed[1, i])
        out_ref[i, 0] = first
        out_ref[i, 1] = second

    for copy in z_own + z_ctr + s_copies + lefts:
        copy.wait_send()

    @pl.loop(0, row_count)
    def _(i):
        square_copy(i).wait_send()
        for n, peer in enumerate(peers):
            out_copy(i, n, peer).wait_send()


def local(grid_size, rep_size, task_blocks, block_cols, task_slot):
    row_count, slots_here, size, _ = task_blocks.shape
    pairs = rep_size
    pad = -(-row_count // 8) * 8
    slot_count = block_cols.shape[1]
    i32 = jnp.int32
    half = size // 2
    f32, bf16 = jnp.float32, jnp.bfloat16
    dma = pltpu.SemaphoreType.DMA
    return pl.pallas_call(
        functools.partial(kernel, grid_size),
        out_shape=jax.ShapeDtypeStruct(task_blocks.shape, f32),
        in_specs=[
            pl.BlockSpec(memory_space=pltpu.HBM),
            pl.BlockSpec(memory_space=pltpu.HBM),
            pl.BlockSpec(memory_space=pltpu.HBM),
        ],
        out_specs=pl.BlockSpec(memory_space=pltpu.VMEM),
        scratch_shapes=[
            pltpu.VMEM(block_cols.shape, i32),
            pltpu.VMEM(block_cols.shape, i32),
            pltpu.SMEM(block_cols.shape, i32),
            pltpu.SMEM(block_cols.shape, i32),
            pltpu.VMEM((3 * pad, slot_count), i32),
            pltpu.VMEM((3 * pad, slot_count), i32),
            pltpu.VMEM((3 * pad, 128), i32),
            pltpu.SMEM((3 * pad, 128), i32),
            pltpu.VMEM((row_count, slots_here, size, size), f32),
            pltpu.VMEM((row_count, size, size), f32),
            pltpu.VMEM((rep_size, row_count, slots_here, half, size), f32),
            pltpu.VMEM((3, rep_size, row_count, size, size), f32),
            pltpu.VMEM((3 * rep_size * row_count, size, size), bf16),
            pltpu.VMEM((3 * rep_size * row_count, size, size), bf16),
            pltpu.VMEM((2, row_count, pairs, half, size), f32),
            pltpu.VMEM((row_count, pairs, half, size), f32),
            pltpu.VMEM((2, row_count, size, size), f32),
            dma, dma((5,)), dma((4,)), dma((4,)), dma, dma, dma((6,)), dma((6,)),
            dma((3,)), dma((3,)), dma((row_count,)), dma((row_count,)),
            dma((3, row_count)), dma((3, row_count)),
        ],
        compiler_params=pltpu.CompilerParams(
            collective_id=0, has_side_effects=True, vmem_limit_bytes=62 * 1024 * 1024
        ),
    )(task_blocks, block_cols, task_slot)


def solution(mesh):
    return jax.shard_map(
        functools.partial(local, mesh.shape["grid"], mesh.shape["rep"]),
        mesh=mesh,
        in_specs=(P(("grp", "grid"), "rep", None, None), P("grp", None), P("grp", None)),
        out_specs=P(("grp", "grid"), "rep", None, None),
        check_vma=False,
    )
```

```python
import functools

import jax
import jax.numpy as jnp
from jax import lax
from jax.experimental import pallas as pl
from jax.experimental.pallas import tpu as pltpu
from jax.sharding import PartitionSpec as P

MESH = pl.DeviceIdType.MESH


def kernel(
    grid_size, task_ref, cols_ref, slots_ref, out_ref,
    cols, slots, cols_smem, slots_smem, codes_vmem, codes,
    own, stage, left, near, near_hi, near_lo, square, out_stage, landed,
    task_sem, meta_sem, z_send, z_recv, x_send, x_recv, s_send, s_recv,
    l_send, l_recv, q_send, q_recv, o_send, o_recv,
):
    row_count, _, size, _ = own.shape
    half = size // 2
    slot_count = 2 * left.shape[0]
    grid_place = lax.axis_index("grid")
    rep = lax.axis_index("rep")
    side = rep // 2
    part = rep % 2
    sib = 2 * side + 1 - part
    ctr = 2 * (1 - side) + part
    diag = 2 * (1 - side) + 1 - part
    up = lax.rem(grid_place + 1, grid_size)
    down = lax.rem(grid_place + grid_size - 1, grid_size)

    def remote(src, dst, send, recv, **where):
        return pltpu.make_async_remote_copy(
            src_ref=src, dst_ref=dst, send_sem=send, recv_sem=recv,
            device_id=where, device_id_type=MESH,
        )

    fetch = pltpu.make_async_copy(task_ref, own, task_sem)
    fetch.start()
    meta = [
        pltpu.make_async_copy(src, dst, meta_sem.at[n])
        for n, (src, dst) in enumerate((
            (cols_ref, cols), (slots_ref, slots), (cols_ref, cols_smem), (slots_ref, slots_smem)
        ))
    ]
    for copy in meta:
        copy.start()
    barrier = pltpu.get_barrier_semaphore()
    for where in ({"grid": up}, {"grid": down}, {"rep": sib}, {"rep": ctr}, {"rep": diag}):
        pl.semaphore_signal(barrier, inc=1, device_id=where, device_id_type=MESH)
    fetch.wait()

    low_lanes = lax.broadcasted_iota(jnp.int32, (size, size), 1) < half

    def swap(first, second):
        low = low_lanes[: first.shape[0]]
        return (
            jnp.where(low, first, pltpu.roll(second, half, 1)),
            jnp.where(low, pltpu.roll(first, half, 1), second),
        )

    @pl.loop(0, row_count)
    def _(i):
        packed = swap(own[i, 0], own[i, 1])
        near[1, rep, i] = jnp.where(side == 0, packed[0], packed[1])
        stage[i] = jnp.where(side == 0, packed[1], packed[0])

    pl.semaphore_wait(barrier, 5)

    to_ctr = remote(stage, near.at[1, rep], x_send, x_recv, rep=ctr)
    to_ctr.start()

    def z_copy(n, source):
        return remote(
            near.at[1, source], near.at[2 * (n % 2), source],
            z_send.at[n], z_recv.at[n], grid=up if n % 2 == 0 else down,
        )

    z_own = [z_copy(n, rep) for n in (0, 1)]
    for copy in z_own:
        copy.start()

    def s_copy(n, direction, source):
        return remote(
            near.at[direction, source], near.at[direction, source],
            s_send.at[n], s_recv.at[n], rep=sib,
        )

    s_copies = [
        s_copy(0, 1, rep), s_copy(1, 1, ctr), s_copy(2, 0, rep),
        s_copy(3, 2, rep), s_copy(4, 0, ctr), s_copy(5, 2, ctr),
    ]
    s_copies[0].start()

    def left_rows(which):
        return own.at[:, :, pl.ds(pl.multiple_of(which * half, half), half), :]

    lefts = [
        remote(left_rows(1 - part), left.at[rep], l_send.at[0], l_recv.at[0], rep=sib),
        remote(left_rows(part), left.at[rep], l_send.at[1], l_recv.at[1], rep=ctr),
        remote(left_rows(1 - part), left.at[rep], l_send.at[2], l_recv.at[2], rep=diag),
    ]
    lefts[0].start()

    @pl.loop(0, row_count)
    def _(i):
        for n in range(2):
            left[rep, i, n] = own[i, n, pl.ds(pl.multiple_of(part * half, half), half), :]

    def split(value):
        high = value.astype(jnp.bfloat16)
        return high, (value - high.astype(jnp.float32)).astype(jnp.bfloat16)

    def convert(direction, source):
        base = (direction * (slot_count // 2) + source) * row_count

        @pl.loop(0, row_count)
        def _(i):
            high, low = split(near[direction, source, i])
            near_hi[base + i] = high
            near_lo[base + i] = low

    for copy in meta:
        copy.wait()
    block_total = row_count * grid_size
    first_row = row_count * (grid_place - 1)
    rows = lax.broadcasted_iota(jnp.int32, cols.shape, 1)
    slot_ids = lax.broadcasted_iota(jnp.int32, cols.shape, 0)
    place = rows - first_row
    place = jnp.where(place < 0, place + block_total, place)
    place = jnp.where(place >= block_total, place - block_total, place)
    tile = (place // row_count) * (slot_count // 2) * row_count + place % row_count
    by_col, by_task = cols[...], slots[...]
    coded = jnp.zeros(cols.shape, jnp.int32)
    for t in range(slot_count):
        coded += jnp.where(
            by_task[t : t + 1] == slot_ids, 4 * (tile + (t // 2) * row_count) + t % 2 - 2, 0
        )
    for i in range(row_count):
        mine = jnp.sum(
            jnp.where(rows == row_count * grid_place + i, by_col, 0), axis=1, keepdims=True
        )
        found = jnp.full(cols.shape, 2, jnp.int32)
        for n in range(slot_count):
            found += jnp.where(by_col[n : n + 1] == mine, coded[n : n + 1], 0)
        codes_vmem[i * slot_count : (i + 1) * slot_count, : cols.shape[1]] = jnp.clip(
            found, 0, 4 * near_hi.shape[0] - 1
        )
    to_smem = pltpu.make_async_copy(codes_vmem, codes, meta_sem.at[4])
    to_smem.start()
    convert(1, rep)
    to_smem.wait()
    to_ctr.wait_recv()
    z_ctr = [z_copy(n, ctr) for n in (2, 3)]
    for copy in z_ctr:
        copy.start()
    s_copies[1].start()
    to_ctr.wait_send()
    lefts[1].start()
    lefts[2].start()
    convert(1, ctr)
    s_copies[0].wait_recv()
    convert(1, sib)
    s_copies[1].wait_recv()
    convert(1, diag)
    for copy, onward, direction in zip(z_own, s_copies[2:4], (0, 2)):
        copy.wait_recv()
        onward.start()
        convert(direction, rep)
    for onward, direction in zip(s_copies[2:4], (0, 2)):
        onward.wait_recv()
        convert(direction, sib)
    for copy in lefts:
        copy.wait_recv()
    for copy, onward, direction in zip(z_ctr, s_copies[4:6], (0, 2)):
        copy.wait_recv()
        onward.start()
        convert(direction, ctr)
    for onward, direction in zip(s_copies[4:6], (0, 2)):
        onward.wait_recv()
        convert(direction, diag)

    lane_half = lax.broadcasted_iota(jnp.int32, (size, size), 1) // half
    nothing = jnp.zeros((size, size), jnp.bfloat16)

    def left_col(i, s, in_task_order):
        row = row_count * grid_place + i
        return cols_smem[slots_smem[s, row] if in_task_order else s, row]

    def products(places, i, pair, lhs):
        total = jnp.zeros((half, 2 * size), jnp.float32)
        for s in range(0, slot_count, 2):
            highs, lows = [], []
            for t in (s, s + 1):
                high_row, low_row = [], []
                for m in range(2):
                    code = codes[i * slot_count + 2 * pair + m, places[t]]
                    tile = code // 4
                    keep = lane_half == code % 4
                    high_row.append(jnp.where(keep, near_hi[tile], nothing))
                    low_row.append(jnp.where(keep, near_lo[tile], nothing))
                highs.append(jnp.concatenate(high_row, axis=1))
                lows.append(jnp.concatenate(low_row, axis=1))
            both = lhs[:, s * size : (s + 2) * size]
            wide = jnp.dot(
                both, jnp.concatenate(highs, axis=0), preferred_element_type=jnp.float32
            )
            total += wide[:half] + wide[half:] + jnp.dot(
                both[:half], jnp.concatenate(lows, axis=0), preferred_element_type=jnp.float32
            )
        first, second = total[:, :size], total[:, size:]
        return jnp.where(
            low_lanes[:half], first + pltpu.roll(first, half, 1), second + pltpu.roll(second, half, 1)
        )

    def left_operand(tiles):
        high, low = split(jnp.concatenate(tiles, axis=1))
        return jnp.concatenate([high, low], axis=0)

    def square_copy(i):
        return remote(
            square.at[side, i], square.at[side, i], q_send.at[i], q_recv.at[i], rep=ctr
        )

    @pl.loop(0, row_count)
    def _(i):
        places = [left_col(i, s, True) for s in range(slot_count)]
        lhs = left_operand([left[t // 2, i, t % 2] for t in range(slot_count)])
        for pair in range(slot_count // 2):
            square[side, i, pair] = products(places, i, pair, lhs)
        square_copy(i).start()

    def out_copy(i, n, peer):
        return remote(
            out_stage.at[i, peer],
            landed.at[side, i, pl.ds(pl.multiple_of(part * half, half), half), :],
            o_send.at[n, i], o_recv.at[n, i], rep=peer,
        )

    peers = (diag, ctr, sib)

    @pl.loop(0, row_count)
    def _(i):
        square_copy(i).wait_recv()
        places = [left_col(i, s, False) for s in range(slot_count)]
        tiles = []
        for pair in range(slot_count // 2):
            tiles.extend(swap(square[0, i, pair], square[1, i, pair]))
        lhs = left_operand(tiles)
        for pair in range(slot_count // 2):
            cubed = products(places, i, pair, lhs)
            out_stage[i, pair] = 3.0 * square[side, i, pair] - 2.0 * cubed
        for n, peer in enumerate(peers):
            out_copy(i, n, peer).start()
        landed[side, i, pl.ds(pl.multiple_of(part * half, half), half), :] = out_stage[i, rep]

    @pl.loop(0, row_count)
    def _(i):
        for n, peer in enumerate(peers):
            out_copy(i, n, peer).wait_recv()
        first, second = swap(landed[0, i], landed[1, i])
        out_ref[i, 0] = first
        out_ref[i, 1] = second

    for copy in z_own + z_ctr + s_copies + lefts:
        copy.wait_send()

    @pl.loop(0, row_count)
    def _(i):
        square_copy(i).wait_send()
        for n, peer in enumerate(peers):
            out_copy(i, n, peer).wait_send()


def local(grid_size, rep_size, task_blocks, block_cols, task_slot):
    row_count, slots_here, size, _ = task_blocks.shape
    pairs = rep_size
    block_cols, task_slot = block_cols.T, task_slot.T
    slot_count, block_total = block_cols.shape
    lanes = -(-block_total // 128) * 128
    i32 = jnp.int32
    half = size // 2
    f32, bf16 = jnp.float32, jnp.bfloat16
    dma = pltpu.SemaphoreType.DMA
    return pl.pallas_call(
        functools.partial(kernel, grid_size),
        out_shape=jax.ShapeDtypeStruct(task_blocks.shape, f32),
        in_specs=[
            pl.BlockSpec(memory_space=pltpu.HBM),
            pl.BlockSpec(memory_space=pltpu.HBM),
            pl.BlockSpec(memory_space=pltpu.HBM),
        ],
        out_specs=pl.BlockSpec(memory_space=pltpu.VMEM),
        scratch_shapes=[
            pltpu.VMEM(block_cols.shape, i32),
            pltpu.VMEM(block_cols.shape, i32),
            pltpu.SMEM(block_cols.shape, i32),
            pltpu.SMEM(block_cols.shape, i32),
            pltpu.VMEM((row_count * slot_count, lanes), i32),
            pltpu.SMEM((row_count * slot_count, lanes), i32),
            pltpu.VMEM((row_count, slots_here, size, size), f32),
            pltpu.VMEM((row_count, size, size), f32),
            pltpu.VMEM((rep_size, row_count, slots_here, half, size), f32),
            pltpu.VMEM((3, rep_size, row_count, size, size), f32),
            pltpu.VMEM((3 * rep_size * row_count, size, size), bf16),
            pltpu.VMEM((3 * rep_size * row_count, size, size), bf16),
            pltpu.VMEM((2, row_count, pairs, half, size), f32),
            pltpu.VMEM((row_count, pairs, half, size), f32),
            pltpu.VMEM((2, row_count, size, size), f32),
            dma, dma((5,)), dma((4,)), dma((4,)), dma, dma, dma((6,)), dma((6,)),
            dma((3,)), dma((3,)), dma((row_count,)), dma((row_count,)),
            dma((3, row_count)), dma((3, row_count)),
        ],
        compiler_params=pltpu.CompilerParams(
            collective_id=0, has_side_effects=True, vmem_limit_bytes=62 * 1024 * 1024
        ),
    )(task_blocks, block_cols, task_slot)


def solution(mesh):
    return jax.shard_map(
        functools.partial(local, mesh.shape["grid"], mesh.shape["rep"]),
        mesh=mesh,
        in_specs=(P(("grp", "grid"), "rep", None, None), P("grp", None), P("grp", None)),
        out_specs=P(("grp", "grid"), "rep", None, None),
        check_vma=False,
    )
```

```python
import functools

import jax
import jax.numpy as jnp
from jax import lax
from jax.experimental import pallas as pl
from jax.experimental.pallas import tpu as pltpu
from jax.sharding import PartitionSpec as P

MESH = pl.DeviceIdType.MESH


def kernel(
    grid_size, task_ref, cols_ref, slots_ref, out_ref,
    cols, slots, cols_smem, slots_smem, codes_vmem, codes,
    own, stage, left, near, near_hi, near_lo, square, out_stage, landed,
    task_sem, meta_sem, z_send, z_recv, x_send, x_recv, s_send, s_recv,
    l_send, l_recv, q_send, q_recv, o_send, o_recv, store_sem,
):
    row_count, _, size, _ = own.shape
    half = size // 2
    slot_count = 2 * left.shape[0]
    grid_place = lax.axis_index("grid")
    rep = lax.axis_index("rep")
    side = rep // 2
    part = rep % 2
    sib = 2 * side + 1 - part
    ctr = 2 * (1 - side) + part
    diag = 2 * (1 - side) + 1 - part
    up = lax.rem(grid_place + 1, grid_size)
    down = lax.rem(grid_place + grid_size - 1, grid_size)

    def remote(src, dst, send, recv, **where):
        return pltpu.make_async_remote_copy(
            src_ref=src, dst_ref=dst, send_sem=send, recv_sem=recv,
            device_id=where, device_id_type=MESH,
        )

    fetch = pltpu.make_async_copy(task_ref, own, task_sem)
    fetch.start()
    meta = [
        pltpu.make_async_copy(src, dst, meta_sem.at[n])
        for n, (src, dst) in enumerate((
            (cols_ref, cols), (slots_ref, slots), (cols_ref, cols_smem), (slots_ref, slots_smem)
        ))
    ]
    for copy in meta:
        copy.start()
    barrier = pltpu.get_barrier_semaphore()
    for where in ({"grid": up}, {"grid": down}, {"rep": sib}, {"rep": ctr}, {"rep": diag}):
        pl.semaphore_signal(barrier, inc=1, device_id=where, device_id_type=MESH)
    fetch.wait()

    low_lanes = lax.broadcasted_iota(jnp.int32, (size, size), 1) < half

    def swap(first, second):
        low = low_lanes[: first.shape[0]]
        return (
            jnp.where(low, first, pltpu.roll(second, half, 1)),
            jnp.where(low, pltpu.roll(first, half, 1), second),
        )

    @pl.loop(0, row_count)
    def _(i):
        packed = swap(own[i, 0], own[i, 1])
        near[1, rep, i] = jnp.where(side == 0, packed[0], packed[1])
        stage[i] = jnp.where(side == 0, packed[1], packed[0])

    pl.semaphore_wait(barrier, 5)

    to_ctr = remote(stage, near.at[1, rep], x_send, x_recv, rep=ctr)
    to_ctr.start()

    def z_copy(n, source):
        return remote(
            near.at[1, source], near.at[2 * (n % 2), source],
            z_send.at[n], z_recv.at[n], grid=up if n % 2 == 0 else down,
        )

    z_own = [z_copy(n, rep) for n in (0, 1)]
    for copy in z_own:
        copy.start()

    def s_copy(n, direction, source):
        return remote(
            near.at[direction, source], near.at[direction, source],
            s_send.at[n], s_recv.at[n], rep=sib,
        )

    s_copies = [
        s_copy(0, 1, rep), s_copy(1, 1, ctr), s_copy(2, 0, rep),
        s_copy(3, 2, rep), s_copy(4, 0, ctr), s_copy(5, 2, ctr),
    ]
    s_copies[0].start()

    def left_rows(which):
        return own.at[:, :, pl.ds(pl.multiple_of(which * half, half), half), :]

    lefts = [
        remote(left_rows(1 - part), left.at[rep], l_send.at[0], l_recv.at[0], rep=sib),
        remote(left_rows(part), left.at[rep], l_send.at[1], l_recv.at[1], rep=ctr),
        remote(left_rows(1 - part), left.at[rep], l_send.at[2], l_recv.at[2], rep=diag),
    ]
    lefts[0].start()

    @pl.loop(0, row_count)
    def _(i):
        for n in range(2):
            left[rep, i, n] = own[i, n, pl.ds(pl.multiple_of(part * half, half), half), :]

    def split(value):
        high = value.astype(jnp.bfloat16)
        return high, (value - high.astype(jnp.float32)).astype(jnp.bfloat16)

    def convert(direction, source):
        base = (direction * (slot_count // 2) + source) * row_count

        @pl.loop(0, row_count)
        def _(i):
            high, low = split(near[direction, source, i])
            near_hi[base + i] = high
            near_lo[base + i] = low

    for copy in meta:
        copy.wait()
    block_total = row_count * grid_size
    first_row = row_count * (grid_place - 1)
    rows = lax.broadcasted_iota(jnp.int32, cols.shape, 1)
    slot_ids = lax.broadcasted_iota(jnp.int32, cols.shape, 0)
    place = rows - first_row
    place = jnp.where(place < 0, place + block_total, place)
    place = jnp.where(place >= block_total, place - block_total, place)
    tile = (place // row_count) * (slot_count // 2) * row_count + place % row_count
    by_col, by_task = cols[...], slots[...]
    coded = jnp.zeros(cols.shape, jnp.int32)
    for t in range(slot_count):
        coded += jnp.where(
            by_task[t : t + 1] == slot_ids, 4 * (tile + (t // 2) * row_count) + t % 2 - 2, 0
        )
    for i in range(row_count):
        mine = jnp.sum(
            jnp.where(rows == row_count * grid_place + i, by_col, 0), axis=1, keepdims=True
        )
        found = jnp.full(cols.shape, 2, jnp.int32)
        for n in range(slot_count):
            found += jnp.where(by_col[n : n + 1] == mine, coded[n : n + 1], 0)
        codes_vmem[i * slot_count : (i + 1) * slot_count, : cols.shape[1]] = jnp.clip(
            found, 0, 4 * near_hi.shape[0] - 1
        )
    to_smem = pltpu.make_async_copy(codes_vmem, codes, meta_sem.at[4])
    to_smem.start()
    convert(1, rep)
    to_smem.wait()
    to_ctr.wait_recv()
    z_ctr = [z_copy(n, ctr) for n in (2, 3)]
    for copy in z_ctr:
        copy.start()
    s_copies[1].start()
    to_ctr.wait_send()
    lefts[1].start()
    lefts[2].start()
    convert(1, ctr)
    s_copies[0].wait_recv()
    convert(1, sib)
    s_copies[1].wait_recv()
    convert(1, diag)
    for copy, onward, direction in zip(z_own, s_copies[2:4], (0, 2)):
        copy.wait_recv()
        onward.start()
        convert(direction, rep)
    for onward, direction in zip(s_copies[2:4], (0, 2)):
        onward.wait_recv()
        convert(direction, sib)
    for copy in lefts:
        copy.wait_recv()
    for copy, onward, direction in zip(z_ctr, s_copies[4:6], (0, 2)):
        copy.wait_recv()
        onward.start()
        convert(direction, ctr)
    for onward, direction in zip(s_copies[4:6], (0, 2)):
        onward.wait_recv()
        convert(direction, diag)

    lane_half = lax.broadcasted_iota(jnp.int32, (size, size), 1) // half
    nothing = jnp.zeros((size, size), jnp.bfloat16)

    def left_col(i, s, in_task_order):
        row = row_count * grid_place + i
        return cols_smem[slots_smem[s, row] if in_task_order else s, row]

    def products(places, i, pair, lhs):
        total = jnp.zeros((half, 2 * size), jnp.float32)
        for s in range(0, slot_count, 2):
            highs, lows = [], []
            for t in (s, s + 1):
                high_row, low_row = [], []
                for m in range(2):
                    code = codes[i * slot_count + 2 * pair + m, places[t]]
                    tile = code // 4
                    keep = lane_half == code % 4
                    high_row.append(jnp.where(keep, near_hi[tile], nothing))
                    low_row.append(jnp.where(keep, near_lo[tile], nothing))
                highs.append(jnp.concatenate(high_row, axis=1))
                lows.append(jnp.concatenate(low_row, axis=1))
            both = lhs[:, s * size : (s + 2) * size]
            wide = jnp.dot(
                both, jnp.concatenate(highs, axis=0), preferred_element_type=jnp.float32
            )
            total += wide[:half] + wide[half:] + jnp.dot(
                both[:half], jnp.concatenate(lows, axis=0), preferred_element_type=jnp.float32
            )
        first, second = total[:, :size], total[:, size:]
        return jnp.where(
            low_lanes[:half], first + pltpu.roll(first, half, 1), second + pltpu.roll(second, half, 1)
        )

    def left_operand(tiles):
        high, low = split(jnp.concatenate(tiles, axis=1))
        return jnp.concatenate([high, low], axis=0)

    def square_copy(i):
        return remote(
            square.at[side, i], square.at[side, i], q_send.at[i], q_recv.at[i], rep=ctr
        )

    @pl.loop(0, row_count)
    def _(i):
        places = [left_col(i, s, True) for s in range(slot_count)]
        lhs = left_operand([left[t // 2, i, t % 2] for t in range(slot_count)])
        for pair in range(slot_count // 2):
            square[side, i, pair] = products(places, i, pair, lhs)
        square_copy(i).start()

    def out_copy(i, n, peer):
        return remote(
            out_stage.at[i, peer],
            landed.at[side, i, pl.ds(pl.multiple_of(part * half, half), half), :],
            o_send.at[n, i], o_recv.at[n, i], rep=peer,
        )

    peers = (diag, ctr, sib)

    @pl.loop(0, row_count)
    def _(i):
        square_copy(i).wait_recv()
        places = [left_col(i, s, False) for s in range(slot_count)]
        tiles = []
        for pair in range(slot_count // 2):
            tiles.extend(swap(square[0, i, pair], square[1, i, pair]))
        lhs = left_operand(tiles)
        for pair in range(slot_count // 2):
            cubed = products(places, i, pair, lhs)
            out_stage[i, pair] = 3.0 * square[side, i, pair] - 2.0 * cubed
        for n, peer in enumerate(peers):
            out_copy(i, n, peer).start()
        landed[side, i, pl.ds(pl.multiple_of(part * half, half), half), :] = out_stage[i, rep]

    for copy in z_own + z_ctr + s_copies + lefts:
        copy.wait_send()

    def store(i):
        return pltpu.make_async_copy(own.at[i], out_ref.at[i], store_sem.at[i])

    @pl.loop(0, row_count)
    def _(i):
        for n, peer in enumerate(peers):
            out_copy(i, n, peer).wait_recv()
        first, second = swap(landed[0, i], landed[1, i])
        own[i, 0] = first
        own[i, 1] = second
        store(i).start()

    @pl.loop(0, row_count)
    def _(i):
        store(i).wait()
        square_copy(i).wait_send()
        for n, peer in enumerate(peers):
            out_copy(i, n, peer).wait_send()


def local(grid_size, rep_size, task_blocks, block_cols, task_slot):
    row_count, slots_here, size, _ = task_blocks.shape
    pairs = rep_size
    block_cols, task_slot = block_cols.T, task_slot.T
    slot_count, block_total = block_cols.shape
    lanes = -(-block_total // 128) * 128
    i32 = jnp.int32
    half = size // 2
    f32, bf16 = jnp.float32, jnp.bfloat16
    dma = pltpu.SemaphoreType.DMA
    return pl.pallas_call(
        functools.partial(kernel, grid_size),
        out_shape=jax.ShapeDtypeStruct(task_blocks.shape, f32),
        in_specs=[
            pl.BlockSpec(memory_space=pltpu.HBM),
            pl.BlockSpec(memory_space=pltpu.HBM),
            pl.BlockSpec(memory_space=pltpu.HBM),
        ],
        out_specs=pl.BlockSpec(memory_space=pltpu.HBM),
        scratch_shapes=[
            pltpu.VMEM(block_cols.shape, i32),
            pltpu.VMEM(block_cols.shape, i32),
            pltpu.SMEM(block_cols.shape, i32),
            pltpu.SMEM(block_cols.shape, i32),
            pltpu.VMEM((row_count * slot_count, lanes), i32),
            pltpu.SMEM((row_count * slot_count, lanes), i32),
            pltpu.VMEM((row_count, slots_here, size, size), f32),
            pltpu.VMEM((row_count, size, size), f32),
            pltpu.VMEM((rep_size, row_count, slots_here, half, size), f32),
            pltpu.VMEM((3, rep_size, row_count, size, size), f32),
            pltpu.VMEM((3 * rep_size * row_count, size, size), bf16),
            pltpu.VMEM((3 * rep_size * row_count, size, size), bf16),
            pltpu.VMEM((2, row_count, pairs, half, size), f32),
            pltpu.VMEM((row_count, pairs, half, size), f32),
            pltpu.VMEM((2, row_count, size, size), f32),
            dma, dma((5,)), dma((4,)), dma((4,)), dma, dma, dma((6,)), dma((6,)),
            dma((3,)), dma((3,)), dma((row_count,)), dma((row_count,)),
            dma((3, row_count)), dma((3, row_count)), dma((row_count,)),
        ],
        compiler_params=pltpu.CompilerParams(
            collective_id=0, has_side_effects=True, vmem_limit_bytes=62 * 1024 * 1024
        ),
    )(task_blocks, block_cols, task_slot)


def solution(mesh):
    return jax.shard_map(
        functools.partial(local, mesh.shape["grid"], mesh.shape["rep"]),
        mesh=mesh,
        in_specs=(P(("grp", "grid"), "rep", None, None), P("grp", None), P("grp", None)),
        out_specs=P(("grp", "grid"), "rep", None, None),
        check_vma=False,
    )
```
